32 devices in a mesh: ctx: 16 (over z, y, core), mp: 2 (over x).
Axes of the slice: x: 2, y: 2, z: 4, core: 2. Of those that a mesh axis runs over, the one named last changes fastest.
Arguments:
- proj: bfloat16 [4096, 3, 8192], P(('ctx', 'mp')), may hold values from -6 to 6
- conv_weight: float32 [3, 7, 8192], replicated, may hold values from -2 to 2
- residues: float32 [128, 16], P('mp'), may hold values from -1.5 to 1.5
- decays: float32 [128, 16], P('mp'), may hold values from 2.4414063e-05 to 0.03
- doc_lengths: int32 [32], replicated, may hold values from 1 to 768, 4096 in all
Outputs:
- mixed: bfloat16 [4096, 8192], P(('ctx', 'mp'))
The draws below stay inside these ranges and needn't reach their ends.
All inputs are finite; a program needn't handle non-finite values.
Results may differ from the reference program's by a relative error of at most 0.014.
Values may be sent and summed in bfloat16 or wider, within the bound.
A program may use at most 128 MiB of HBM per device.

```python
import math
import jax
import jax.numpy as jnp
import numpy as np
from jax import lax

D = 8192
GSIZE = 64
MODES = 16
KERNEL = 7
TOK_DEV = 256
GROUPS = 128
TOKENS = 4096
DOCS = 32


def level_of(rng, shape, cuts, least, high):
    def one(position, parts):
        heights = jax.random.uniform(jax.random.fold_in(jax.random.fold_in(rng, 6), position), (parts,), jnp.float32, least / len(cuts), high / len(cuts))
        return jnp.repeat(jnp.exp(heights), shape[position] // parts).reshape((-1,) + (1,) * (len(shape) - position - 1))

    loudness = one(*cuts[0])
    for cut in cuts[1:]:
        loudness = loudness * one(*cut)
    return loudness


def length_profile(amount, total, bound, slope):
    weights = [(1 << 20) // math.isqrt(rank ** slope) + 1 for rank in range(2, amount + 1)]
    spare, counts = total - bound - (amount - 1), [1] * (amount - 1)
    while spare > 0:
        candidates = [i for i in range(amount - 1) if counts[i] < bound]
        pool, remaining = sum([weights[i] for i in candidates]), spare
        for i in candidates:
            extra = min(bound - counts[i], max(1, remaining * weights[i] // pool), spare)
            counts[i] = counts[i] + extra
            spare = spare - extra
    return np.array([bound] + counts)


def ragged_sizes(key, number_of, total, most, skew):
    if number_of == 2:
        one = jax.random.randint(key, (), max(1, total - most), min(most, total - 1) + 1)
        return jnp.stack([one, total - one])
    sizes = jnp.asarray(length_profile(number_of, total, most, skew), jnp.int32)
    couples = (number_of - 1) // 2
    donor, receiver = sizes[1:1 + 2 * couples:2], sizes[2:2 + 2 * couples:2]
    room = jnp.minimum(donor - 1, most - receiver)
    shifted = jax.random.randint(jax.random.fold_in(key, 1), (couples,), 0, 1 << 20) % (room + 1)
    sizes = sizes.at[1:1 + 2 * couples:2].set(donor - shifted).at[2:2 + 2 * couples:2].set(receiver + shifted)
    return sizes[jax.random.permutation(jax.random.fold_in(key, 2), number_of)]


def normal_values(own_key, shape, deviation, bound, shards=(), held_as=jnp.bfloat16):
    values = deviation * jax.random.normal(own_key, shape, jnp.float32)
    if shards:
        values = values * level_of(own_key, shape, shards, -0.22, 0.18)
    return jnp.clip(values, -bound, bound).astype(held_as)


def setup_inputs(seed: int = 0) -> dict:
    splits = jax.random.split(jax.random.key(seed), 6)
    proj = normal_values(splits[0], (TOKENS, 3, D), 1.0, 6.0, ((0, 32),))
    conv_weight = normal_values(splits[1], (3, KERNEL, D), 0.4, 2.0, (), jnp.float32)
    residues = normal_values(splits[2], (GROUPS, MODES), 0.25, 1.5, ((0, 2),), jnp.float32)
    decays = jnp.clip(jnp.exp(math.log(0.03) - 7.1137933 * jax.random.uniform(splits[3], (GROUPS, MODES), jnp.float32) ** level_of(splits[3], (GROUPS, MODES), ((0, 2),), -0.2, 0.2)), 2.441406286379788e-05, 0.03)
    doc_lengths = ragged_sizes(splits[4], DOCS, TOKENS, 3 * TOK_DEV, 1).astype(jnp.int32)
    return dict(proj=proj, conv_weight=conv_weight, residues=residues, decays=decays, doc_lengths=doc_lengths)


def document_number_index(doc_lengths, positions):
    doc_starts = jnp.cumsum(doc_lengths) - doc_lengths
    inside = (doc_starts[None, :] <= positions[:, None]).astype(jnp.int32)
    return (lax.optimization_barrier(jnp.sum(inside, axis=1)) - 1).astype(jnp.int32)

def short_convolution(padded, conv_weight, padded_document_ids, padded_pos, out_rows):
    kernel_len = conv_weight.shape[1]
    result = jnp.zeros((out_rows,) + padded.shape[1:], jnp.float32)
    own_docs = padded_document_ids[kernel_len - 1:]
    for position_shift in range(kernel_len):
        begin_row = kernel_len - 1 - position_shift
        earlier = padded[begin_row:begin_row + out_rows].astype(jnp.float32)
        keep_mask = (padded_document_ids[begin_row:begin_row + out_rows] == own_docs) & (padded_pos[begin_row:begin_row + out_rows] >= 0)
        result = result + conv_weight[:, position_shift, :][None] * earlier * keep_mask.astype(jnp.float32)[:, None, None]
    return result

def filter_taps(residues, decays, lag_values):
    coefficient = residues * jnp.sqrt(decays)
    powers = jnp.exp(-decays[:, :, None] * lag_values[None, None, :])
    return jnp.einsum('gm,gmt->gt', coefficient, powers, precision=lax.Precision.HIGHEST)

def reference(proj, conv_weight, residues, decays, doc_lengths):
    padded_pos = (jnp.arange(TOKENS + KERNEL - 1) - (KERNEL - 1)).astype(jnp.int32)
    padded_document_ids = document_number_index(doc_lengths, padded_pos)
    padded = jnp.pad(proj, ((KERNEL - 1, 0), (0, 0), (0, 0)))
    conv = short_convolution(padded, conv_weight, padded_document_ids, padded_pos, TOKENS)
    query_part = conv[:, 0]
    product = (conv[:, 1] * conv[:, 2]).astype(jnp.bfloat16)
    lag_values = jnp.arange(TOKENS).astype(jnp.float32)
    tap_table = filter_taps(residues, decays, lag_values)
    grouped = product.astype(jnp.float32).reshape(TOKENS, GROUPS, GSIZE).transpose(1, 0, 2)

    def one_group(group_pair):
        tap_row, inputs = group_pair
        length = 2 * TOKENS
        spectrum = jnp.fft.rfft(tap_row, length)[:, None] * jnp.fft.rfft(inputs, length, axis=0)
        return jnp.fft.irfft(spectrum, length, axis=0)[:TOKENS].astype(jnp.float32)
    filtered = lax.map(one_group, (tap_table, grouped))
    filtered = filtered.transpose(1, 0, 2).reshape(TOKENS, D).astype(jnp.bfloat16)
    return (query_part * filtered.astype(jnp.float32)).astype(jnp.bfloat16)
```

```python
import functools

import jax
import jax.numpy as jnp
from jax import lax
from jax.experimental import pallas as pl
from jax.experimental.pallas import tpu as pltpu
from jax.sharding import PartitionSpec as P

LANES = 128
HALO = 8
AXES = ("ctx", "mp")
F32 = jnp.float32
BF16 = jnp.bfloat16


def rows_since_start(doc_lengths, positions):
    order = jnp.arange(doc_lengths.shape[0])
    ahead = order[None, :] < order[:, None]
    starts = jnp.sum(jnp.where(ahead, doc_lengths[None, :], 0), axis=1)
    begun = starts[None, :] <= positions[:, None]
    return positions - jnp.max(jnp.where(begun, starts[None, :], 0), axis=1)


def lag_lanes(rows):
    return lax.broadcasted_iota(jnp.int32, (rows, LANES), 1)


def conv_tile(window, x_ref, halo_ref, w_ref, mask_ref, j, columns):
    taps, rows = w_ref.shape[1], x_ref.shape[1]
    window[:HALO] = halo_ref[j, :, columns].astype(F32)
    window[HALO:] = x_ref[j, :, columns].astype(F32)
    total = w_ref[j, 0:1, columns] * window[HALO:]
    for k in range(1, taps):
        earlier = window[HALO - k : HALO - k + rows] * mask_ref[k]
        total = total + w_ref[j, k : k + 1, columns] * earlier
    return total


def group_rows(ref, group, modes):
    return ref[group * modes : (group + 1) * modes]


def state_kernel(modes, x_ref, halo_ref, w_ref, mask_ref, decay_ref, u_ref, state_ref, win_k, win_v):
    rows = x_ref.shape[1]
    left = lag_lanes(modes) < LANES // 2
    ages = (rows - 1 - lag_lanes(modes)).astype(F32)
    for tile in range(x_ref.shape[2] // LANES):
        columns = slice(tile * LANES, (tile + 1) * LANES)
        keys = conv_tile(win_k, x_ref, halo_ref, w_ref, mask_ref, 0, columns)
        values = conv_tile(win_v, x_ref, halo_ref, w_ref, mask_ref, 1, columns)
        u = (keys * values).astype(BF16)
        u_ref[:, columns] = u
        halves = []
        for side in range(2):
            decay = group_rows(decay_ref, 2 * tile + side, modes)
            weight = jnp.exp(-decay * ages).astype(BF16)[:, :rows]
            halves.append(jnp.dot(weight, u, preferred_element_type=F32))
        state_ref[:, columns] = jnp.where(left, halves[0], halves[1]).astype(BF16)


def prefix_kernel(rows, r_ref, decay_ref, p_ref):
    devices = r_ref.shape[0]
    step = jnp.exp(-decay_ref[...] * float(rows))

    def body(j, carry):
        p_ref[j] = carry.astype(BF16)
        return step * carry + r_ref[j].astype(F32)

    lax.fori_loop(0, devices, body, jnp.zeros(r_ref.shape[1:], F32))


def mix_kernel(modes, x_ref, halo_ref, w_ref, mask_ref, decay_ref, coef_ref, u_ref, carry_ref, o_ref, win_q):
    rows = x_ref.shape[1]
    left = lag_lanes(rows) < LANES // 2
    lane = lag_lanes(modes)
    after = (lane + 1).astype(F32)
    back = jnp.where(lane == 0, 0, LANES - lane).astype(F32)
    causal = lag_lanes(rows) <= lax.broadcasted_iota(jnp.int32, (rows, LANES), 0)
    for tile in range(x_ref.shape[2] // LANES):
        columns = slice(tile * LANES, (tile + 1) * LANES)
        query = conv_tile(win_q, x_ref, halo_ref, w_ref, mask_ref, 0, columns)
        u = u_ref[:, columns]
        carry = carry_ref[:, columns]
        halves = []
        for side in range(2):
            decay = group_rows(decay_ref, 2 * tile + side, modes)
            coef = group_rows(coef_ref, 2 * tile + side, modes)
            into = (coef * jnp.exp(-decay * after)).astype(BF16)[:, :rows]
            taps = jnp.sum(coef * jnp.exp(-decay * back), axis=0, keepdims=True)
            spread = pltpu.roll(jnp.broadcast_to(taps, (rows, LANES)), 0, 1, stride=1, stride_axis=0)
            local = jnp.where(causal, spread, 0.0).astype(BF16)[:, :rows]
            half = jnp.dot(local, u, preferred_element_type=F32)
            half += lax.dot_general(into, carry, (((0,), (0,)), ((), ())), preferred_element_type=F32)
            halves.append(half)
        z = jnp.where(left, halves[0], halves[1]).astype(BF16).astype(F32)
        o_ref[:, columns] = (query * z).astype(BF16)


def everywhere(block, axis):
    n = lax.axis_size(axis)
    copies = jnp.broadcast_to(block[None], (n,) + block.shape)
    return lax.all_to_all(copies, axis, 0, 0, tiled=True).reshape((-1,) + block.shape[1:])


def shards(proj, conv_weight, residues, decays, doc_lengths):
    rows, _, width = proj.shape
    taps = conv_weight.shape[1]
    modes = residues.shape[1]
    devices = lax.axis_size("ctx") * lax.axis_size("mp")
    me = lax.axis_index("ctx") * lax.axis_size("mp") + lax.axis_index("mp")

    x = proj.transpose(1, 0, 2)
    halo = lax.ppermute(x[:, rows - HALO :], AXES, [(i, i + 1) for i in range(devices - 1)])
    both = everywhere(jnp.concatenate([residues, decays], axis=1), "mp")
    residues, decays = both[:, :modes], both[:, modes:]
    groups = residues.shape[0]
    coef = (residues * jnp.sqrt(decays)).reshape(-1, 1)
    coef = jnp.broadcast_to(coef, (groups * modes, LANES))
    decay = jnp.broadcast_to(decays.reshape(-1, 1), (groups * modes, LANES))
    since = rows_since_start(doc_lengths, me * rows + jnp.arange(rows, dtype=jnp.int32))
    mask = (since[None, :] >= jnp.arange(taps)[:, None]).astype(F32)
    mask = jnp.broadcast_to(mask[:, :, None], (taps, rows, LANES))

    block = 512
    per = modes * groups * block // width
    row_block = lambda n: pl.BlockSpec((n, block), lambda i: (0, i))
    whole_mask = pl.BlockSpec(mask.shape, lambda i: (0, 0, 0))
    mode_block = pl.BlockSpec((per, LANES), lambda i: (i, 0))
    window = pltpu.VMEM((rows + HALO, LANES), F32)
    params = pltpu.CompilerParams(vmem_limit_bytes=48 * 2**20)

    def three(n, a, j):
        return pl.BlockSpec((a, n, block), lambda i: (j, 0, i))

    u, state = pl.pallas_call(
        functools.partial(state_kernel, modes),
        grid=(width // block,),
        out_shape=(jax.ShapeDtypeStruct((rows, width), BF16), jax.ShapeDtypeStruct((modes, width), BF16)),
        in_specs=[three(rows, 2, 0), three(HALO, 2, 0), three(taps, 2, 0), whole_mask, mode_block],
        out_specs=(row_block(rows), row_block(modes)),
        scratch_shapes=[window, window],
        compiler_params=params,
    )(x[1:], halo[1:], conv_weight[1:], mask, decay)

    share = width // devices
    sent = state.reshape(modes, devices, share).transpose(1, 0, 2)
    received = lax.all_to_all(sent, AXES, 0, 0, tiled=True)
    channel = me * share + jnp.arange(share, dtype=jnp.int32)
    my_decay = jnp.take(decays, channel // (width // groups), axis=0).T
    before = pl.pallas_call(
        functools.partial(prefix_kernel, rows),
        out_shape=jax.ShapeDtypeStruct((devices, modes, share), BF16),
        compiler_params=params,
    )(received, my_decay)
    carry = lax.all_to_all(before, AXES, 0, 0, tiled=True)
    carry = carry.transpose(1, 0, 2).reshape(modes, width)

    return pl.pallas_call(
        functools.partial(mix_kernel, modes),
        grid=(width // block,),
        out_shape=jax.ShapeDtypeStruct((rows, width), BF16),
        in_specs=[
            three(rows, 1, 0),
            three(HALO, 1, 0),
            three(taps, 1, 0),
            whole_mask,
            mode_block,
            mode_block,
            row_block(rows),
            row_block(modes),
        ],
        out_specs=row_block(rows),
        scratch_shapes=[window],
        compiler_params=params,
    )(x, halo, conv_weight, mask, decay, coef, u, carry)


def solution(mesh):
    return jax.shard_map(
        shards,
        mesh=mesh,
        in_specs=(P(AXES, None, None), P(), P("mp", None), P("mp", None), P()),
        out_specs=P(AXES, None),
        check_vma=False,
    )
```

```python
import functools

import jax
import jax.numpy as jnp
from jax import lax
from jax.experimental import pallas as pl
from jax.experimental.pallas import tpu as pltpu
from jax.sharding import PartitionSpec as P

LANES = 128
HALO = 8
UNROLL = 2
AXES = ("ctx", "mp")
F32 = jnp.float32
BF16 = jnp.bfloat16


def rows_since_start(doc_lengths, positions):
    order = jnp.arange(doc_lengths.shape[0])
    ahead = order[None, :] < order[:, None]
    starts = jnp.sum(jnp.where(ahead, doc_lengths[None, :], 0), axis=1)
    begun = starts[None, :] <= positions[:, None]
    return positions - jnp.max(jnp.where(begun, starts[None, :], 0), axis=1)


def lag_lanes(rows):
    return lax.broadcasted_iota(jnp.int32, (rows, LANES), 1)


def conv_tiles(windows, x_ref, halo_ref, w_ref, mask_ref, parts, columns):
    taps, rows = w_ref.shape[1], x_ref.shape[1]
    chunk = min(rows, 64)
    for window, j in zip(windows, parts):
        window[:HALO] = halo_ref[j, :, columns].astype(F32)
        window[HALO:] = x_ref[j, :, columns].astype(F32)
    pieces = [[] for _ in parts]
    for first in range(0, rows, chunk):
        totals = [
            w_ref[j, 0:1, columns] * window[HALO + first : HALO + first + chunk]
            for window, j in zip(windows, parts)
        ]
        for k in range(1, taps):
            keep = mask_ref[k, first : first + chunk]
            start = HALO - k + first
            for i, j in enumerate(parts):
                earlier = windows[i][start : start + chunk] * keep
                totals[i] = totals[i] + w_ref[j, k : k + 1, columns] * earlier
        for i, total in enumerate(totals):
            pieces[i].append(total)
    return [jnp.concatenate(p, axis=0) for p in pieces]


def mixer_kernel(
    sizes,
    x_ref,
    halo_ref,
    w_ref,
    mask_ref,
    decay_ref,
    coef_ref,
    my_decay_ref,
    o_ref,
    u_ref,
    y_ref,
    q_ref,
    state_ref,
    carry_ref,
    seen_ref,
    before_ref,
    wins,
    local_sem,
    send_sems,
    recv_sems,
):
    modes, devices, mp, share, stride = sizes
    rows, width = x_ref.shape[1:]
    owners = width // share
    me = lax.axis_index("ctx") * mp + lax.axis_index("mp")
    tiles = width // LANES
    pair = 2 * modes

    def peer(i):
        other = lax.rem(me + i, devices)
        return other, (other // mp, lax.rem(other, mp))

    barrier = pltpu.get_barrier_semaphore()

    @pl.loop(1, devices)
    def _(i):
        pl.semaphore_signal(barrier, inc=1, device_id=peer(i)[1], device_id_type=pl.DeviceIdType.MESH)

    left = lag_lanes(modes) < LANES // 2
    lane = lag_lanes(pair)
    ages = (rows - 1 - lane).astype(F32)

    def cols(tile):
        return pl.ds(pl.multiple_of(tile * LANES, LANES), LANES)

    def mode_rows(ref, tile):
        return ref[pl.ds(pl.multiple_of(tile * pair, pair), pair)]

    @pl.loop(0, tiles // UNROLL)
    def _(step):
        for part in range(UNROLL):
            tile = step * UNROLL + part
            columns = cols(tile)
            two = [wins.at[2 * part], wins.at[2 * part + 1]]
            keys, values = conv_tiles(two, x_ref, halo_ref, w_ref, mask_ref, (1, 2), columns)
            u = (keys * values).astype(BF16)
            u_ref[:, columns] = u
            weight = jnp.exp(-mode_rows(decay_ref, tile) * ages).astype(BF16)[:, :rows]
            sums = jnp.dot(weight, u, preferred_element_type=F32)
            state_ref[:, columns] = jnp.where(left, sums[:modes], sums[modes:]).astype(BF16)

    pl.semaphore_wait(barrier, devices - 1)

    def share_of(index):
        return pl.ds(pl.multiple_of(index * share, share), share)

    def is_owner(index):
        return lax.rem(index, stride) == 0

    def when(always, condition):
        return (lambda f: f()) if always else pl.when(condition)

    @pl.loop(1, devices)
    def _(i):
        other, where = peer(i)

        @when(stride == 1, is_owner(other))
        def _():
            pltpu.make_async_remote_copy(
                state_ref.at[:, share_of(other // stride)],
                seen_ref.at[me],
                send_sems.at[0],
                recv_sems.at[0],
                device_id=where,
                device_id_type=pl.DeviceIdType.MESH,
            ).start()

    @when(stride == 1, is_owner(me))
    def _():
        own = pltpu.make_async_copy(state_ref.at[:, share_of(me // stride)], seen_ref.at[me], local_sem)
        own.start()
        own.wait()

    wide_left = lag_lanes(rows) < LANES // 2
    back = jnp.where(lane == 0, 0, LANES - lane).astype(F32)
    causal = lag_lanes(rows) <= lax.broadcasted_iota(jnp.int32, (rows, LANES), 0)

    @pl.loop(0, tiles // UNROLL)
    def _(step):
        for part in range(UNROLL):
            tile = step * UNROLL + part
            columns = cols(tile)
            (query,) = conv_tiles([wins.at[2 * part]], x_ref, halo_ref, w_ref, mask_ref, (0,), columns)
            q_ref[:, columns] = query
            u = u_ref[:, columns]
            terms = mode_rows(coef_ref, tile) * jnp.exp(-mode_rows(decay_ref, tile) * back)
            halves = []
            for side in range(2):
                taps = jnp.sum(terms[side * modes : (side + 1) * modes], axis=0, keepdims=True)
                spread = pltpu.roll(jnp.broadcast_to(taps, (rows, LANES)), 0, 1, stride=1, stride_axis=0)
                local = jnp.where(causal, spread, 0.0).astype(BF16)[:, :rows]
                halves.append(jnp.dot(local, u, preferred_element_type=F32))
            y_ref[:, columns] = jnp.where(wide_left, halves[0], halves[1])

    @when(stride == 1, is_owner(me))
    def _():
        others = seen_ref.at[pl.ds(0, devices - 1)]
        pltpu.make_async_copy(others, others, recv_sems.at[0]).wait()
        decayed = jnp.exp(-my_decay_ref[...] * float(rows))

        def body(j, carry):
            before_ref[j] = carry.astype(BF16)
            return decayed * carry + seen_ref[j].astype(F32)

        lax.fori_loop(0, devices, body, jnp.zeros(seen_ref.shape[1:], F32))

        @pl.loop(1, devices)
        def _(i):
            other, where = peer(i)
            pltpu.make_async_remote_copy(
                before_ref.at[other],
                carry_ref.at[:, share_of(me // stride)],
                send_sems.at[1],
                recv_sems.at[1],
                device_id=where,
                device_id_type=pl.DeviceIdType.MESH,
            ).start()

        own = pltpu.make_async_copy(before_ref.at[me], carry_ref.at[:, share_of(me // stride)], local_sem)
        own.start()
        own.wait()

    def wait_shares(sem, count):
        some = carry_ref.at[:, pl.ds(0, count * share)]
        pltpu.make_async_copy(some, some, sem).wait()

    if stride == 1:
        wait_shares(send_sems.at[0], owners - 1)
        wait_shares(recv_sems.at[1], owners - 1)
    else:

        @pl.when(is_owner(me))
        def _():
            wait_shares(send_sems.at[0], owners - 1)
            wait_shares(recv_sems.at[1], owners - 1)

        @pl.when(jnp.logical_not(is_owner(me)))
        def _():
            wait_shares(send_sems.at[0], owners)
            wait_shares(recv_sems.at[1], owners)

    after = (lane + 1).astype(F32)
    @pl.loop(0, tiles // UNROLL)
    def _(step):
        for part in range(UNROLL):
            tile = step * UNROLL + part
            columns = cols(tile)
            into = (mode_rows(coef_ref, tile) * jnp.exp(-mode_rows(decay_ref, tile) * after)).astype(BF16)[:, :rows]
            carry = carry_ref[:, columns].astype(F32)
            split = jnp.concatenate([jnp.where(left, carry, 0.0), jnp.where(left, 0.0, carry)], axis=0)
            gained = lax.dot_general(into, split.astype(BF16), (((0,), (0,)), ((), ())), preferred_element_type=F32)
            z = (y_ref[:, columns] + gained).astype(BF16).astype(F32)
            o_ref[:, columns] = (q_ref[:, columns] * z).astype(BF16)

    @when(stride == 1, is_owner(me))
    def _():
        others = before_ref.at[pl.ds(0, devices - 1)]
        pltpu.make_async_copy(others, others, send_sems.at[1]).wait()


def everywhere(block, axis):
    n = lax.axis_size(axis)
    copies = jnp.broadcast_to(block[None], (n,) + block.shape)
    return lax.all_to_all(copies, axis, 0, 0, tiled=True).reshape((-1,) + block.shape[1:])


def shards(proj, conv_weight, residues, decays, doc_lengths):
    rows, _, width = proj.shape
    taps = conv_weight.shape[1]
    modes = residues.shape[1]
    devices = lax.axis_size("ctx") * lax.axis_size("mp")
    me = lax.axis_index("ctx") * lax.axis_size("mp") + lax.axis_index("mp")

    x = proj.transpose(1, 0, 2)
    halo = lax.ppermute(x[:, rows - HALO :], AXES, [(i, i + 1) for i in range(devices - 1)])
    both = everywhere(jnp.concatenate([residues, decays], axis=1), "mp")
    residues, decays = both[:, :modes], both[:, modes:]
    groups = residues.shape[0]
    coef = (residues * jnp.sqrt(decays)).reshape(-1, 1)
    coef = jnp.broadcast_to(coef, (groups * modes, LANES))
    decay = jnp.broadcast_to(decays.reshape(-1, 1), (groups * modes, LANES))
    since = rows_since_start(doc_lengths, me * rows + jnp.arange(rows, dtype=jnp.int32))
    mask = (since[None, :] >= jnp.arange(taps)[:, None]).astype(F32)
    mask = jnp.broadcast_to(mask[:, :, None], (taps, rows, LANES))

    mp = lax.axis_size("mp")
    share = max(width // devices, LANES)
    stride = devices * share // width
    channel = (me // stride) * share + jnp.arange(share, dtype=jnp.int32)
    my_decay = jnp.take(decays, channel // (width // groups), axis=0).T
    in_vmem = pl.BlockSpec(memory_space=pltpu.VMEM)
    return pl.pallas_call(
        functools.partial(mixer_kernel, (modes, devices, mp, share, stride)),
        out_shape=jax.ShapeDtypeStruct((rows, width), BF16),
        in_specs=[in_vmem] * 7,
        out_specs=in_vmem,
        scratch_shapes=[
            pltpu.VMEM((rows, width), BF16),
            pltpu.VMEM((rows, width), F32),
            pltpu.VMEM((rows, width), F32),
            pltpu.VMEM((modes, width), BF16),
            pltpu.VMEM((modes, width), BF16),
            pltpu.VMEM((devices, modes, share), BF16),
            pltpu.VMEM((devices, modes, share), BF16),
            pltpu.VMEM((2 * UNROLL, rows + HALO, LANES), F32),
            pltpu.SemaphoreType.DMA,
            pltpu.SemaphoreType.DMA((2,)),
            pltpu.SemaphoreType.DMA((2,)),
        ],
        compiler_params=pltpu.CompilerParams(
            collective_id=0, has_side_effects=True, vmem_limit_bytes=48 * 2**20
        ),
    )(x, halo, conv_weight, mask, decay, coef, my_decay)


def solution(mesh):
    return jax.shard_map(
        shards,
        mesh=mesh,
        in_specs=(P(AXES, None, None), P(), P("mp", None), P("mp", None), P()),
        out_specs=P(AXES, None),
        check_vma=False,
    )
```

```python
import functools

import jax
import jax.numpy as jnp
from jax import lax
from jax.experimental import pallas as pl
from jax.experimental.pallas import tpu as pltpu
from jax.sharding import PartitionSpec as P

LANES = 128
HALO = 8
UNROLL = 4
AXES = ("ctx", "mp")
F32 = jnp.float32
BF16 = jnp.bfloat16


def rows_since_start(doc_lengths, positions):
    order = jnp.arange(doc_lengths.shape[0])
    ahead = order[None, :] < order[:, None]
    starts = jnp.sum(jnp.where(ahead, doc_lengths[None, :], 0), axis=1)
    begun = starts[None, :] <= positions[:, None]
    return positions - jnp.max(jnp.where(begun, starts[None, :], 0), axis=1)


def lag_lanes(rows):
    return lax.broadcasted_iota(jnp.int32, (rows, LANES), 1)


def conv_tiles(windows, x_ref, halo_ref, w_ref, mask_ref, parts, columns):
    taps, rows = w_ref.shape[1], x_ref.shape[1]
    chunk = min(rows, 64)
    for window, j in zip(windows, parts):
        window[:HALO] = halo_ref[j, :, columns].astype(F32)
        window[HALO:] = x_ref[j, :, columns].astype(F32)
    pieces = [[] for _ in parts]
    for first in range(0, rows, chunk):
        totals = [
            w_ref[j, 0:1, columns] * window[HALO + first : HALO + first + chunk]
            for window, j in zip(windows, parts)
        ]
        for k in range(1, taps):
            keep = mask_ref[k, first : first + chunk]
            start = HALO - k + first
            for i, j in enumerate(parts):
                earlier = windows[i][start : start + chunk] * keep
                totals[i] = totals[i] + w_ref[j, k : k + 1, columns] * earlier
        for i, total in enumerate(totals):
            pieces[i].append(total)
    return [jnp.concatenate(p, axis=0) for p in pieces]


def mixer_kernel(
    sizes,
    x_ref,
    halo_ref,
    w_ref,
    mask_ref,
    decay_ref,
    coef_ref,
    my_decay_ref,
    o_ref,
    u_ref,
    y_ref,
    q_ref,
    state_ref,
    carry_ref,
    seen_ref,
    before_ref,
    wins,
    local_sem,
    send_sems,
    recv_sems,
):
    modes, devices, mp, share, stride = sizes
    rows, width = x_ref.shape[1:]
    owners = width // share
    me = lax.axis_index("ctx") * mp + lax.axis_index("mp")
    tiles = width // LANES
    pair = 2 * modes

    def peer(i):
        other = lax.rem(me + i, devices)
        return other, (other // mp, lax.rem(other, mp))

    barrier = pltpu.get_barrier_semaphore()

    @pl.loop(1, devices)
    def _(i):
        pl.semaphore_signal(barrier, inc=1, device_id=peer(i)[1], device_id_type=pl.DeviceIdType.MESH)

    left = lag_lanes(modes) < LANES // 2
    lane = lag_lanes(pair)
    ages = (rows - 1 - lane).astype(F32)

    def cols(tile):
        return pl.ds(pl.multiple_of(tile * LANES, LANES), LANES)

    def mode_rows(ref, tile):
        return ref[pl.ds(pl.multiple_of(tile * pair, pair), pair)]

    @pl.loop(0, tiles // UNROLL)
    def _(step):
        for part in range(UNROLL):
            tile = step * UNROLL + part
            columns = cols(tile)
            two = [wins.at[2 * part], wins.at[2 * part + 1]]
            keys, values = conv_tiles(two, x_ref, halo_ref, w_ref, mask_ref, (1, 2), columns)
            u = (keys * values).astype(BF16)
            u_ref[:, columns] = u
            weight = jnp.exp(-mode_rows(decay_ref, tile) * ages).astype(BF16)[:, :rows]
            sums = jnp.dot(weight, u, preferred_element_type=F32)
            state_ref[:, columns] = jnp.where(left, sums[:modes], sums[modes:]).astype(BF16)

    pl.semaphore_wait(barrier, devices - 1)

    def share_of(index):
        return pl.ds(pl.multiple_of(index * share, share), share)

    def is_owner(index):
        return lax.rem(index, stride) == 0

    def when(always, condition):
        return (lambda f: f()) if always else pl.when(condition)

    @pl.loop(1, devices)
    def _(i):
        other, where = peer(i)

        @when(stride == 1, is_owner(other))
        def _():
            pltpu.make_async_remote_copy(
                state_ref.at[:, share_of(other // stride)],
                seen_ref.at[me],
                send_sems.at[0],
                recv_sems.at[0],
                device_id=where,
                device_id_type=pl.DeviceIdType.MESH,
            ).start()

    @when(stride == 1, is_owner(me))
    def _():
        own = pltpu.make_async_copy(state_ref.at[:, share_of(me // stride)], seen_ref.at[me], local_sem)
        own.start()
        own.wait()

    wide_left = lag_lanes(rows) < LANES // 2
    back = jnp.where(lane == 0, 0, LANES - lane).astype(F32)
    causal = lag_lanes(rows) <= lax.broadcasted_iota(jnp.int32, (rows, LANES), 0)

    @pl.loop(0, tiles // UNROLL)
    def _(step):
        for part in range(UNROLL):
            tile = step * UNROLL + part
            columns = cols(tile)
            (query,) = conv_tiles([wins.at[2 * part]], x_ref, halo_ref, w_ref, mask_ref, (0,), columns)
            q_ref[:, columns] = query
            u = u_ref[:, columns]
            terms = mode_rows(coef_ref, tile) * jnp.exp(-mode_rows(decay_ref, tile) * back)
            halves = []
            for side in range(2):
                taps = jnp.sum(terms[side * modes : (side + 1) * modes], axis=0, keepdims=True)
                spread = pltpu.roll(jnp.broadcast_to(taps, (rows, LANES)), 0, 1, stride=1, stride_axis=0)
                local = jnp.where(causal, spread, 0.0).astype(BF16)[:, :rows]
                halves.append(jnp.dot(local, u, preferred_element_type=F32))
            y_ref[:, columns] = jnp.where(wide_left, halves[0], halves[1])

    @when(stride == 1, is_owner(me))
    def _():
        others = seen_ref.at[pl.ds(0, devices - 1)]
        pltpu.make_async_copy(others, others, recv_sems.at[0]).wait()
        decayed = jnp.exp(-my_decay_ref[...] * float(rows))

        def body(j, carry):
            before_ref[j] = carry.astype(BF16)
            return decayed * carry + seen_ref[j].astype(F32)

        lax.fori_loop(0, devices, body, jnp.zeros(seen_ref.shape[1:], F32))

        @pl.loop(1, devices)
        def _(i):
            other, where = peer(i)
            pltpu.make_async_remote_copy(
                before_ref.at[other],
                carry_ref.at[:, share_of(me // stride)],
                send_sems.at[1],
                recv_sems.at[1],
                device_id=where,
                device_id_type=pl.DeviceIdType.MESH,
            ).start()

        own = pltpu.make_async_copy(before_ref.at[me], carry_ref.at[:, share_of(me // stride)], local_sem)
        own.start()
        own.wait()

    def wait_shares(sem, count):
        some = carry_ref.at[:, pl.ds(0, count * share)]
        pltpu.make_async_copy(some, some, sem).wait()

    if stride == 1:
        wait_shares(send_sems.at[0], owners - 1)
        wait_shares(recv_sems.at[1], owners - 1)
    else:

        @pl.when(is_owner(me))
        def _():
            wait_shares(send_sems.at[0], owners - 1)
            wait_shares(recv_sems.at[1], owners - 1)

        @pl.when(jnp.logical_not(is_owner(me)))
        def _():
            wait_shares(send_sems.at[0], owners)
            wait_shares(recv_sems.at[1], owners)

    after = (lane + 1).astype(F32)
    @pl.loop(0, tiles // UNROLL)
    def _(step):
        for part in range(UNROLL):
            tile = step * UNROLL + part
            columns = cols(tile)
            into = (mode_rows(coef_ref, tile) * jnp.exp(-mode_rows(decay_ref, tile) * after)).astype(BF16)[:, :rows]
            carry = carry_ref[:, columns].astype(F32)
            split = jnp.concatenate([jnp.where(left, carry, 0.0), jnp.where(left, 0.0, carry)], axis=0)
            gained = lax.dot_general(into, split.astype(BF16), (((0,), (0,)), ((), ())), preferred_element_type=F32)
            z = (y_ref[:, columns] + gained).astype(BF16).astype(F32)
            o_ref[:, columns] = (q_ref[:, columns] * z).astype(BF16)

    @when(stride == 1, is_owner(me))
    def _():
        others = before_ref.at[pl.ds(0, devices - 1)]
        pltpu.make_async_copy(others, others, send_sems.at[1]).wait()


def everywhere(block, axis):
    n = lax.axis_size(axis)
    me = lax.axis_index(axis)
    gathered = jnp.zeros((n,) + block.shape, block.dtype)
    gathered = lax.dynamic_update_index_in_dim(gathered, block, me, 0)
    for shift in range(1, n):
        arrived = lax.ppermute(block, axis, [(i, (i + shift) % n) for i in range(n)])
        source = lax.rem(me - shift + n, n)
        gathered = lax.dynamic_update_index_in_dim(gathered, arrived, source, 0)
    return gathered.reshape((-1,) + block.shape[1:])


def shards(proj, conv_weight, residues, decays, doc_lengths):
    rows, _, width = proj.shape
    taps = conv_weight.shape[1]
    modes = residues.shape[1]
    devices = lax.axis_size("ctx") * lax.axis_size("mp")
    me = lax.axis_index("ctx") * lax.axis_size("mp") + lax.axis_index("mp")

    x = proj.transpose(1, 0, 2)
    halo = lax.ppermute(x[:, rows - HALO :], AXES, [(i, i + 1) for i in range(devices - 1)])
    both = everywhere(jnp.concatenate([residues, decays], axis=1), "mp")
    residues, decays = both[:, :modes], both[:, modes:]
    groups = residues.shape[0]
    coef = (residues * jnp.sqrt(decays)).reshape(-1, 1)
    coef = jnp.broadcast_to(coef, (groups * modes, LANES))
    decay = jnp.broadcast_to(decays.reshape(-1, 1), (groups * modes, LANES))
    since = rows_since_start(doc_lengths, me * rows + jnp.arange(rows, dtype=jnp.int32))
    mask = (since[None, :] >= jnp.arange(taps)[:, None]).astype(F32)
    mask = jnp.broadcast_to(mask[:, :, None], (taps, rows, LANES))

    mp = lax.axis_size("mp")
    share = max(width // devices, LANES)
    stride = devices * share // width
    channel = (me // stride) * share + jnp.arange(share, dtype=jnp.int32)
    my_decay = jnp.take(decays, channel // (width // groups), axis=0).T
    in_vmem = pl.BlockSpec(memory_space=pltpu.VMEM)
    return pl.pallas_call(
        functools.partial(mixer_kernel, (modes, devices, mp, share, stride)),
        out_shape=jax.ShapeDtypeStruct((rows, width), BF16),
        in_specs=[in_vmem] * 7,
        out_specs=in_vmem,
        scratch_shapes=[
            pltpu.VMEM((rows, width), BF16),
            pltpu.VMEM((rows, width), F32),
            pltpu.VMEM((rows, width), F32),
            pltpu.VMEM((modes, width), BF16),
            pltpu.VMEM((modes, width), BF16),
            pltpu.VMEM((devices, modes, share), BF16),
            pltpu.VMEM((devices, modes, share), BF16),
            pltpu.VMEM((2 * UNROLL, rows + HALO, LANES), F32),
            pltpu.SemaphoreType.DMA,
            pltpu.SemaphoreType.DMA((2,)),
            pltpu.SemaphoreType.DMA((2,)),
        ],
        compiler_params=pltpu.CompilerParams(
            collective_id=0, has_side_effects=True, vmem_limit_bytes=48 * 2**20
        ),
    )(x, halo, conv_weight, mask, decay, coef, my_decay)


def solution(mesh):
    return jax.shard_map(
        shards,
        mesh=mesh,
        in_specs=(P(AXES, None, None), P(), P("mp", None), P("mp", None), P()),
        out_specs=P(AXES, None),
        check_vma=False,
    )
```

```python
import functools

import jax
import jax.numpy as jnp
from jax import lax
from jax.experimental import pallas as pl
from jax.experimental.pallas import tpu as pltpu
from jax.sharding import PartitionSpec as P

LANES = 128
HALO = 8
UNROLL = 8
AXES = ("ctx", "mp")
F32 = jnp.float32
BF16 = jnp.bfloat16


def rows_since_start(doc_lengths, positions):
    order = jnp.arange(doc_lengths.shape[0])
    ahead = order[None, :] < order[:, None]
    starts = jnp.sum(jnp.where(ahead, doc_lengths[None, :], 0), axis=1)
    begun = starts[None, :] <= positions[:, None]
    return positions - jnp.max(jnp.where(begun, starts[None, :], 0), axis=1)


def lag_lanes(rows):
    return lax.broadcasted_iota(jnp.int32, (rows, LANES), 1)


def conv_tiles(windows, x_ref, halo_ref, w_ref, mask_ref, parts, columns):
    taps, rows = w_ref.shape[1], x_ref.shape[1]
    chunk = min(rows, 64)
    for window, j in zip(windows, parts):
        window[:HALO] = halo_ref[j, :, columns].astype(F32)
        window[HALO:] = x_ref[j, :, columns].astype(F32)
    pieces = [[] for _ in parts]
    for first in range(0, rows, chunk):
        totals = [
            w_ref[j, 0:1, columns] * window[HALO + first : HALO + first + chunk]
            for window, j in zip(windows, parts)
        ]
        for k in range(1, taps):
            keep = mask_ref[k, first : first + chunk]
            start = HALO - k + first
            for i, j in enumerate(parts):
                earlier = windows[i][start : start + chunk] * keep
                totals[i] = totals[i] + w_ref[j, k : k + 1, columns] * earlier
        for i, total in enumerate(totals):
            pieces[i].append(total)
    return [jnp.concatenate(p, axis=0) for p in pieces]


def mixer_kernel(
    sizes,
    x_ref,
    halo_ref,
    w_ref,
    mask_ref,
    decay_ref,
    coef_ref,
    my_decay_ref,
    o_ref,
    u_ref,
    y_ref,
    q_ref,
    state_ref,
    carry_ref,
    seen_ref,
    before_ref,
    wins,
    local_sem,
    send_sems,
    recv_sems,
):
    modes, devices, mp, share, stride = sizes
    rows, width = x_ref.shape[1:]
    owners = width // share
    me = lax.axis_index("ctx") * mp + lax.axis_index("mp")
    tiles = width // LANES
    pair = 2 * modes

    def peer(i):
        other = lax.rem(me + i, devices)
        return other, (other // mp, lax.rem(other, mp))

    barrier = pltpu.get_barrier_semaphore()

    @pl.loop(1, devices)
    def _(i):
        pl.semaphore_signal(barrier, inc=1, device_id=peer(i)[1], device_id_type=pl.DeviceIdType.MESH)

    left = lag_lanes(modes) < LANES // 2
    lane = lag_lanes(pair)
    ages = (rows - 1 - lane).astype(F32)

    def cols(tile):
        return pl.ds(pl.multiple_of(tile * LANES, LANES), LANES)

    def mode_rows(ref, tile):
        return ref[pl.ds(pl.multiple_of(tile * pair, pair), pair)]

    @pl.loop(0, tiles // UNROLL)
    def _(step):
        for part in range(UNROLL):
            tile = step * UNROLL + part
            columns = cols(tile)
            two = [wins.at[2 * part], wins.at[2 * part + 1]]
            keys, values = conv_tiles(two, x_ref, halo_ref, w_ref, mask_ref, (1, 2), columns)
            u = (keys * values).astype(BF16)
            u_ref[:, columns] = u
            weight = jnp.exp(-mode_rows(decay_ref, tile) * ages).astype(BF16)[:, :rows]
            sums = jnp.dot(weight, u, preferred_element_type=F32)
            state_ref[:, columns] = jnp.where(left, sums[:modes], sums[modes:]).astype(BF16)

    pl.semaphore_wait(barrier, devices - 1)

    def share_of(index):
        return pl.ds(pl.multiple_of(index * share, share), share)

    def is_owner(index):
        return lax.rem(index, stride) == 0

    def when(always, condition):
        return (lambda f: f()) if always else pl.when(condition)

    @pl.loop(1, devices)
    def _(i):
        other, where = peer(i)

        @when(stride == 1, is_owner(other))
        def _():
            pltpu.make_async_remote_copy(
                state_ref.at[:, share_of(other // stride)],
                seen_ref.at[me],
                send_sems.at[0],
                recv_sems.at[0],
                device_id=where,
                device_id_type=pl.DeviceIdType.MESH,
            ).start()

    @when(stride == 1, is_owner(me))
    def _():
        own = pltpu.make_async_copy(state_ref.at[:, share_of(me // stride)], seen_ref.at[me], local_sem)
        own.start()
        own.wait()

    wide_left = lag_lanes(rows) < LANES // 2
    back = jnp.where(lane == 0, 0, LANES - lane).astype(F32)
    causal = lag_lanes(rows) <= lax.broadcasted_iota(jnp.int32, (rows, LANES), 0)

    @pl.loop(0, tiles // UNROLL)
    def _(step):
        for part in range(UNROLL):
            tile = step * UNROLL + part
            columns = cols(tile)
            (query,) = conv_tiles([wins.at[2 * part]], x_ref, halo_ref, w_ref, mask_ref, (0,), columns)
            q_ref[:, columns] = query
            u = u_ref[:, columns]
            terms = mode_rows(coef_ref, tile) * jnp.exp(-mode_rows(decay_ref, tile) * back)
            halves = []
            for side in range(2):
                taps = jnp.sum(terms[side * modes : (side + 1) * modes], axis=0, keepdims=True)
                spread = pltpu.roll(jnp.broadcast_to(taps, (rows, LANES)), 0, 1, stride=1, stride_axis=0)
                local = jnp.where(causal, spread, 0.0).astype(BF16)[:, :rows]
                halves.append(jnp.dot(local, u, preferred_element_type=F32))
            y_ref[:, columns] = jnp.where(wide_left, halves[0], halves[1])

    @when(stride == 1, is_owner(me))
    def _():
        others = seen_ref.at[pl.ds(0, devices - 1)]
        pltpu.make_async_copy(others, others, recv_sems.at[0]).wait()
        decayed = jnp.exp(-my_decay_ref[...] * float(rows))

        def body(j, carry):
            before_ref[j] = carry.astype(BF16)
            return decayed * carry + seen_ref[j].astype(F32)

        lax.fori_loop(0, devices, body, jnp.zeros(seen_ref.shape[1:], F32))

        @pl.loop(1, devices)
        def _(i):
            other, where = peer(i)
            pltpu.make_async_remote_copy(
                before_ref.at[other],
                carry_ref.at[:, share_of(me // stride)],
                send_sems.at[1],
                recv_sems.at[1],
                device_id=where,
                device_id_type=pl.DeviceIdType.MESH,
            ).start()

        own = pltpu.make_async_copy(before_ref.at[me], carry_ref.at[:, share_of(me // stride)], local_sem)
        own.start()
        own.wait()

    def wait_shares(sem, count):
        some = carry_ref.at[:, pl.ds(0, count * share)]
        pltpu.make_async_copy(some, some, sem).wait()

    if stride == 1:
        wait_shares(send_sems.at[0], owners - 1)
        wait_shares(recv_sems.at[1], owners - 1)
    else:

        @pl.when(is_owner(me))
        def _():
            wait_shares(send_sems.at[0], owners - 1)
            wait_shares(recv_sems.at[1], owners - 1)

        @pl.when(jnp.logical_not(is_owner(me)))
        def _():
            wait_shares(send_sems.at[0], owners)
            wait_shares(recv_sems.at[1], owners)

    after = (lane + 1).astype(F32)
    @pl.loop(0, tiles // UNROLL)
    def _(step):
        for part in range(UNROLL):
            tile = step * UNROLL + part
            columns = cols(tile)
            into = (mode_rows(coef_ref, tile) * jnp.exp(-mode_rows(decay_ref, tile) * after)).astype(BF16)[:, :rows]
            carry = carry_ref[:, columns].astype(F32)
            split = jnp.concatenate([jnp.where(left, carry, 0.0), jnp.where(left, 0.0, carry)], axis=0)
            gained = lax.dot_general(into, split.astype(BF16), (((0,), (0,)), ((), ())), preferred_element_type=F32)
            z = (y_ref[:, columns] + gained).astype(BF16).astype(F32)
            o_ref[:, columns] = (q_ref[:, columns] * z).astype(BF16)

    @when(stride == 1, is_owner(me))
    def _():
        others = before_ref.at[pl.ds(0, devices - 1)]
        pltpu.make_async_copy(others, others, send_sems.at[1]).wait()


def everywhere(block, axis):
    n = lax.axis_size(axis)
    me = lax.axis_index(axis)
    gathered = jnp.zeros((n,) + block.shape, block.dtype)
    gathered = lax.dynamic_update_index_in_dim(gathered, block, me, 0)
    for shift in range(1, n):
        arrived = lax.ppermute(block, axis, [(i, (i + shift) % n) for i in range(n)])
        source = lax.rem(me - shift + n, n)
        gathered = lax.dynamic_update_index_in_dim(gathered, arrived, source, 0)
    return gathered.reshape((-1,) + block.shape[1:])


def shards(proj, conv_weight, residues, decays, doc_lengths):
    rows, _, width = proj.shape
    taps = conv_weight.shape[1]
    modes = residues.shape[1]
    devices = lax.axis_size("ctx") * lax.axis_size("mp")
    me = lax.axis_index("ctx") * lax.axis_size("mp") + lax.axis_index("mp")

    x = proj.transpose(1, 0, 2)
    halo = lax.ppermute(x[:, rows - HALO :], AXES, [(i, i + 1) for i in range(devices - 1)])
    both = everywhere(jnp.concatenate([residues, decays], axis=1), "mp")
    residues, decays = both[:, :modes], both[:, modes:]
    groups = residues.shape[0]
    coef = (residues * jnp.sqrt(decays)).reshape(-1, 1)
    coef = jnp.broadcast_to(coef, (groups * modes, LANES))
    decay = jnp.broadcast_to(decays.reshape(-1, 1), (groups * modes, LANES))
    since = rows_since_start(doc_lengths, me * rows + jnp.arange(rows, dtype=jnp.int32))
    mask = (since[None, :] >= jnp.arange(taps)[:, None]).astype(F32)
    mask = jnp.broadcast_to(mask[:, :, None], (taps, rows, LANES))

    mp = lax.axis_size("mp")
    share = max(width // devices, LANES)
    stride = devices * share // width
    channel = (me // stride) * share + jnp.arange(share, dtype=jnp.int32)
    my_decay = jnp.take(decays, channel // (width // groups), axis=0).T
    in_vmem = pl.BlockSpec(memory_space=pltpu.VMEM)
    return pl.pallas_call(
        functools.partial(mixer_kernel, (modes, devices, mp, share, stride)),
        out_shape=jax.ShapeDtypeStruct((rows, width), BF16),
        in_specs=[in_vmem] * 7,
        out_specs=in_vmem,
        scratch_shapes=[
            pltpu.VMEM((rows, width), BF16),
            pltpu.VMEM((rows, width), F32),
            pltpu.VMEM((rows, width), F32),
            pltpu.VMEM((modes, width), BF16),
            pltpu.VMEM((modes, width), BF16),
            pltpu.VMEM((devices, modes, share), BF16),
            pltpu.VMEM((devices, modes, share), BF16),
            pltpu.VMEM((2 * UNROLL, rows + HALO, LANES), F32),
            pltpu.SemaphoreType.DMA,
            pltpu.SemaphoreType.DMA((2,)),
            pltpu.SemaphoreType.DMA((2,)),
        ],
        compiler_params=pltpu.CompilerParams(
            collective_id=0, has_side_effects=True, vmem_limit_bytes=48 * 2**20
        ),
    )(x, halo, conv_weight, mask, decay, coef, my_decay)


def solution(mesh):
    return jax.shard_map(
        shards,
        mesh=mesh,
        in_specs=(P(AXES, None, None), P(), P("mp", None), P("mp", None), P()),
        out_specs=P(AXES, None),
        check_vma=False,
    )
```

```python
import functools

import jax
import jax.numpy as jnp
from jax import lax
from jax.experimental import pallas as pl
from jax.experimental.pallas import tpu as pltpu
from jax.sharding import PartitionSpec as P

LANES = 128
HALO = 8
UNROLL = 8
AXES = ("ctx", "mp")
F32 = jnp.float32
BF16 = jnp.bfloat16


def rows_since_start(doc_lengths, positions):
    order = jnp.arange(doc_lengths.shape[0])
    ahead = order[None, :] < order[:, None]
    starts = jnp.sum(jnp.where(ahead, doc_lengths[None, :], 0), axis=1)
    begun = starts[None, :] <= positions[:, None]
    return positions - jnp.max(jnp.where(begun, starts[None, :], 0), axis=1)


def lag_lanes(rows):
    return lax.broadcasted_iota(jnp.int32, (rows, LANES), 1)


def conv_tiles(windows, x_ref, halo_ref, w_ref, mask_ref, parts, columns):
    taps, rows = w_ref.shape[1], x_ref.shape[1]
    chunk = min(rows, 64)
    for window, j in zip(windows, parts):
        window[:HALO] = halo_ref[j, :, columns].astype(F32)
        window[HALO:] = x_ref[j, :, columns].astype(F32)
    pieces = [[] for _ in parts]
    for first in range(0, rows, chunk):
        totals = [
            w_ref[j, 0:1, columns] * window[HALO + first : HALO + first + chunk]
            for window, j in zip(windows, parts)
        ]
        for k in range(1, taps):
            keep = mask_ref[k, first : first + chunk]
            start = HALO - k + first
            for i, j in enumerate(parts):
                earlier = windows[i][start : start + chunk] * keep
                totals[i] = totals[i] + w_ref[j, k : k + 1, columns] * earlier
        for i, total in enumerate(totals):
            pieces[i].append(total)
    return [jnp.concatenate(p, axis=0) for p in pieces]


def mixer_kernel(
    sizes,
    x_ref,
    halo_ref,
    w_ref,
    mask_ref,
    decay_ref,
    coef_ref,
    my_decay_ref,
    o_ref,
    u_ref,
    y_ref,
    q_ref,
    state_ref,
    carry_ref,
    seen_ref,
    before_ref,
    wins,
    local_sem,
    send_sems,
    recv_sems,
):
    modes, devices, mp, share, stride = sizes
    rows, width = x_ref.shape[1:]
    owners = width // share
    me = lax.axis_index("ctx") * mp + lax.axis_index("mp")
    tiles = width // LANES
    pair = 2 * modes

    def peer(i):
        other = lax.rem(me + i, devices)
        return other, (other // mp, lax.rem(other, mp))

    barrier = pltpu.get_barrier_semaphore()

    @pl.loop(1, devices)
    def _(i):
        pl.semaphore_signal(barrier, inc=1, device_id=peer(i)[1], device_id_type=pl.DeviceIdType.MESH)

    left = lag_lanes(modes) < LANES // 2
    lane = lag_lanes(pair)
    ages = (rows - 1 - lane).astype(F32)

    def cols(tile):
        return pl.ds(pl.multiple_of(tile * LANES, LANES), LANES)

    def mode_rows(ref, tile):
        return ref[pl.ds(pl.multiple_of(tile * pair, pair), pair)]

    @pl.loop(0, tiles // UNROLL)
    def _(step):
        for part in range(UNROLL):
            tile = step * UNROLL + part
            columns = cols(tile)
            two = [wins.at[2 * part], wins.at[2 * part + 1]]
            keys, values = conv_tiles(two, x_ref, halo_ref, w_ref, mask_ref, (1, 2), columns)
            u = (keys * values).astype(BF16)
            u_ref[:, columns] = u
            weight = jnp.exp(-mode_rows(decay_ref, tile) * ages).astype(BF16)[:, :rows]
            sums = jnp.dot(weight, u, preferred_element_type=F32)
            state_ref[:, columns] = jnp.where(left, sums[:modes], sums[modes:]).astype(BF16)

    pl.semaphore_wait(barrier, devices - 1)

    def share_of(index):
        return pl.ds(pl.multiple_of(index * share, share), share)

    def is_owner(index):
        return lax.rem(index, stride) == 0

    def when(always, condition):
        return (lambda f: f()) if always else pl.when(condition)

    @pl.loop(1, devices)
    def _(i):
        other, where = peer(i)

        @when(stride == 1, is_owner(other))
        def _():
            pltpu.make_async_remote_copy(
                state_ref.at[:, share_of(other // stride)],
                seen_ref.at[me],
                send_sems.at[0],
                recv_sems.at[0],
                device_id=where,
                device_id_type=pl.DeviceIdType.MESH,
            ).start()

    @when(stride == 1, is_owner(me))
    def _():
        own = pltpu.make_async_copy(state_ref.at[:, share_of(me // stride)], seen_ref.at[me], local_sem)
        own.start()
        own.wait()

    wide_left = lag_lanes(rows) < LANES // 2
    back = jnp.where(lane == 0, 0, LANES - lane).astype(F32)
    causal = lag_lanes(rows) <= lax.broadcasted_iota(jnp.int32, (rows, LANES), 0)

    def local_step(step):
        for part in range(UNROLL):
            tile = step * UNROLL + part
            columns = cols(tile)
            (query,) = conv_tiles([wins.at[2 * part]], x_ref, halo_ref, w_ref, mask_ref, (0,), columns)
            q_ref[:, columns] = query
            u = u_ref[:, columns]
            terms = mode_rows(coef_ref, tile) * jnp.exp(-mode_rows(decay_ref, tile) * back)
            halves = []
            for side in range(2):
                taps = jnp.sum(terms[side * modes : (side + 1) * modes], axis=0, keepdims=True)
                spread = pltpu.roll(jnp.broadcast_to(taps, (rows, LANES)), 0, 1, stride=1, stride_axis=0)
                local = jnp.where(causal, spread, 0.0).astype(BF16)[:, :rows]
                halves.append(jnp.dot(local, u, preferred_element_type=F32))
            y_ref[:, columns] = jnp.where(wide_left, halves[0], halves[1])

    steps = tiles // UNROLL
    pl.loop(0, steps // 2)(local_step)

    @when(stride == 1, is_owner(me))
    def _():
        others = seen_ref.at[pl.ds(0, devices - 1)]
        pltpu.make_async_copy(others, others, recv_sems.at[0]).wait()
        decayed = jnp.exp(-my_decay_ref[...] * float(rows))

        def body(j, carry):
            before_ref[j] = carry.astype(BF16)
            return decayed * carry + seen_ref[j].astype(F32)

        lax.fori_loop(0, devices, body, jnp.zeros(seen_ref.shape[1:], F32))

        @pl.loop(1, devices)
        def _(i):
            other, where = peer(i)
            pltpu.make_async_remote_copy(
                before_ref.at[other],
                carry_ref.at[:, share_of(me // stride)],
                send_sems.at[1],
                recv_sems.at[1],
                device_id=where,
                device_id_type=pl.DeviceIdType.MESH,
            ).start()

        own = pltpu.make_async_copy(before_ref.at[me], carry_ref.at[:, share_of(me // stride)], local_sem)
        own.start()
        own.wait()

    pl.loop(steps // 2, steps)(local_step)

    def wait_shares(sem, count):
        some = carry_ref.at[:, pl.ds(0, count * share)]
        pltpu.make_async_copy(some, some, sem).wait()

    if stride == 1:
        wait_shares(send_sems.at[0], owners - 1)
        wait_shares(recv_sems.at[1], owners - 1)
    else:

        @pl.when(is_owner(me))
        def _():
            wait_shares(send_sems.at[0], owners - 1)
            wait_shares(recv_sems.at[1], owners - 1)

        @pl.when(jnp.logical_not(is_owner(me)))
        def _():
            wait_shares(send_sems.at[0], owners)
            wait_shares(recv_sems.at[1], owners)

    after = (lane + 1).astype(F32)
    @pl.loop(0, tiles // UNROLL)
    def _(step):
        for part in range(UNROLL):
            tile = step * UNROLL + part
            columns = cols(tile)
            into = (mode_rows(coef_ref, tile) * jnp.exp(-mode_rows(decay_ref, tile) * after)).astype(BF16)[:, :rows]
            carry = carry_ref[:, columns].astype(F32)
            split = jnp.concatenate([jnp.where(left, carry, 0.0), jnp.where(left, 0.0, carry)], axis=0)
            gained = lax.dot_general(into, split.astype(BF16), (((0,), (0,)), ((), ())), preferred_element_type=F32)
            z = (y_ref[:, columns] + gained).astype(BF16).astype(F32)
            o_ref[:, columns] = (q_ref[:, columns] * z).astype(BF16)

    @when(stride == 1, is_owner(me))
    def _():
        others = before_ref.at[pl.ds(0, devices - 1)]
        pltpu.make_async_copy(others, others, send_sems.at[1]).wait()


def everywhere(block, axis):
    n = lax.axis_size(axis)
    me = lax.axis_index(axis)
    gathered = jnp.zeros((n,) + block.shape, block.dtype)
    gathered = lax.dynamic_update_index_in_dim(gathered, block, me, 0)
    for shift in range(1, n):
        arrived = lax.ppermute(block, axis, [(i, (i + shift) % n) for i in range(n)])
        source = lax.rem(me - shift + n, n)
        gathered = lax.dynamic_update_index_in_dim(gathered, arrived, source, 0)
    return gathered.reshape((-1,) + block.shape[1:])


def shards(proj, conv_weight, residues, decays, doc_lengths):
    rows, _, width = proj.shape
    taps = conv_weight.shape[1]
    modes = residues.shape[1]
    devices = lax.axis_size("ctx") * lax.axis_size("mp")
    me = lax.axis_index("ctx") * lax.axis_size("mp") + lax.axis_index("mp")

    x = proj.transpose(1, 0, 2)
    halo = lax.ppermute(x[:, rows - HALO :], AXES, [(i, i + 1) for i in range(devices - 1)])
    both = everywhere(jnp.concatenate([residues, decays], axis=1), "mp")
    residues, decays = both[:, :modes], both[:, modes:]
    groups = residues.shape[0]
    coef = (residues * jnp.sqrt(decays)).reshape(-1, 1)
    coef = jnp.broadcast_to(coef, (groups * modes, LANES))
    decay = jnp.broadcast_to(decays.reshape(-1, 1), (groups * modes, LANES))
    since = rows_since_start(doc_lengths, me * rows + jnp.arange(rows, dtype=jnp.int32))
    mask = (since[None, :] >= jnp.arange(taps)[:, None]).astype(F32)
    mask = jnp.broadcast_to(mask[:, :, None], (taps, rows, LANES))

    mp = lax.axis_size("mp")
    share = max(width // devices, LANES)
    stride = devices * share // width
    channel = (me // stride) * share + jnp.arange(share, dtype=jnp.int32)
    my_decay = jnp.take(decays, channel // (width // groups), axis=0).T
    in_vmem = pl.BlockSpec(memory_space=pltpu.VMEM)
    return pl.pallas_call(
        functools.partial(mixer_kernel, (modes, devices, mp, share, stride)),
        out_shape=jax.ShapeDtypeStruct((rows, width), BF16),
        in_specs=[in_vmem] * 7,
        out_specs=in_vmem,
        scratch_shapes=[
            pltpu.VMEM((rows, width), BF16),
            pltpu.VMEM((rows, width), F32),
            pltpu.VMEM((rows, width), F32),
            pltpu.VMEM((modes, width), BF16),
            pltpu.VMEM((modes, width), BF16),
            pltpu.VMEM((devices, modes, share), BF16),
            pltpu.VMEM((devices, modes, share), BF16),
            pltpu.VMEM((2 * UNROLL, rows + HALO, LANES), F32),
            pltpu.SemaphoreType.DMA,
            pltpu.SemaphoreType.DMA((2,)),
            pltpu.SemaphoreType.DMA((2,)),
        ],
        compiler_params=pltpu.CompilerParams(
            collective_id=0, has_side_effects=True, vmem_limit_bytes=48 * 2**20
        ),
    )(x, halo, conv_weight, mask, decay, coef, my_decay)


def solution(mesh):
    return jax.shard_map(
        shards,
        mesh=mesh,
        in_specs=(P(AXES, None, None), P(), P("mp", None), P("mp", None), P()),
        out_specs=P(AXES, None),
        check_vma=False,
    )
```

```python
import functools

import jax
import jax.numpy as jnp
from jax import lax
from jax.experimental import pallas as pl
from jax.experimental.pallas import tpu as pltpu
from jax.sharding import PartitionSpec as P

LANES = 128
HALO = 8
UNROLL = 8
AXES = ("ctx", "mp")
F32 = jnp.float32
BF16 = jnp.bfloat16


def rows_since_start(doc_lengths, positions):
    order = jnp.arange(doc_lengths.shape[0])
    ahead = order[None, :] < order[:, None]
    starts = jnp.sum(jnp.where(ahead, doc_lengths[None, :], 0), axis=1)
    begun = starts[None, :] <= positions[:, None]
    return positions - jnp.max(jnp.where(begun, starts[None, :], 0), axis=1)


def lag_lanes(rows):
    return lax.broadcasted_iota(jnp.int32, (rows, LANES), 1)


def conv_tiles(windows, x_ref, halo_ref, w_ref, mask_ref, parts, columns):
    taps, rows = w_ref.shape[1], x_ref.shape[1]
    chunk = min(rows, 64)
    for window, j in zip(windows, parts):
        window[:HALO] = halo_ref[j, :, columns].astype(F32)
        window[HALO:] = x_ref[j, :, columns].astype(F32)
    pieces = [[] for _ in parts]
    for first in range(0, rows, chunk):
        totals = [
            w_ref[j, 0:1, columns] * window[HALO + first : HALO + first + chunk]
            for window, j in zip(windows, parts)
        ]
        for k in range(1, taps):
            keep = mask_ref[k, first : first + chunk]
            start = HALO - k + first
            for i, j in enumerate(parts):
                earlier = windows[i][start : start + chunk] * keep
                totals[i] = totals[i] + w_ref[j, k : k + 1, columns] * earlier
        for i, total in enumerate(totals):
            pieces[i].append(total)
    return [jnp.concatenate(p, axis=0) for p in pieces]


def mixer_kernel(
    sizes,
    x_ref,
    halo_ref,
    w_ref,
    mask_ref,
    decay_ref,
    coef_ref,
    my_decay_ref,
    o_ref,
    u_ref,
    y_ref,
    q_ref,
    state_ref,
    carry_ref,
    seen_ref,
    before_ref,
    wins,
    local_sem,
    send_sems,
    recv_sems,
):
    modes, devices, mp, share, stride = sizes
    rows, width = x_ref.shape[1:]
    owners = width // share
    me = lax.axis_index("ctx") * mp + lax.axis_index("mp")
    tiles = width // LANES
    pair = 2 * modes

    def peer(i):
        other = lax.rem(me + i, devices)
        return other, (other // mp, lax.rem(other, mp))

    barrier = pltpu.get_barrier_semaphore()

    @pl.loop(1, devices)
    def _(i):
        pl.semaphore_signal(barrier, inc=1, device_id=peer(i)[1], device_id_type=pl.DeviceIdType.MESH)

    left = lag_lanes(modes) < LANES // 2
    lane = lag_lanes(pair)
    ages = (rows - 1 - lane).astype(F32)

    def cols(tile):
        return pl.ds(pl.multiple_of(tile * LANES, LANES), LANES)

    def mode_rows(ref, tile):
        return ref[pl.ds(pl.multiple_of(tile * pair, pair), pair)]

    @pl.loop(0, tiles // UNROLL)
    def _(step):
        for part in range(UNROLL):
            tile = step * UNROLL + part
            columns = cols(tile)
            two = [wins.at[2 * part], wins.at[2 * part + 1]]
            keys, values = conv_tiles(two, x_ref, halo_ref, w_ref, mask_ref, (1, 2), columns)
            u = (keys * values).astype(BF16)
            u_ref[:, columns] = u
            weight = jnp.exp(-mode_rows(decay_ref, tile) * ages).astype(BF16)[:, :rows]
            sums = jnp.dot(weight, u, preferred_element_type=F32)
            state_ref[:, columns] = jnp.where(left, sums[:modes], sums[modes:]).astype(BF16)

    pl.semaphore_wait(barrier, devices - 1)

    def share_of(index):
        return pl.ds(pl.multiple_of(index * share, share), share)

    def is_owner(index):
        return lax.rem(index, stride) == 0

    def when(always, condition):
        return (lambda f: f()) if always else pl.when(condition)

    @pl.loop(1, devices)
    def _(i):
        other, where = peer(i)

        @when(stride == 1, is_owner(other))
        def _():
            pltpu.make_async_remote_copy(
                state_ref.at[:, share_of(other // stride)],
                seen_ref.at[me],
                send_sems.at[0],
                recv_sems.at[0],
                device_id=where,
                device_id_type=pl.DeviceIdType.MESH,
            ).start()

    @when(stride == 1, is_owner(me))
    def _():
        own = pltpu.make_async_copy(state_ref.at[:, share_of(me // stride)], seen_ref.at[me], local_sem)
        own.start()
        own.wait()

    wide_left = lag_lanes(rows) < LANES // 2
    back = jnp.where(lane == 0, 0, LANES - lane).astype(F32)
    causal = lag_lanes(rows) <= lax.broadcasted_iota(jnp.int32, (rows, LANES), 0)

    @pl.loop(0, tiles // UNROLL)
    def _(step):
        for part in range(UNROLL):
            tile = step * UNROLL + part
            columns = cols(tile)
            (query,) = conv_tiles([wins.at[2 * part]], x_ref, halo_ref, w_ref, mask_ref, (0,), columns)
            q_ref[:, columns] = query
            u = u_ref[:, columns]
            terms = mode_rows(coef_ref, tile) * jnp.exp(-mode_rows(decay_ref, tile) * back)
            halves = []
            for side in range(2):
                taps = jnp.sum(terms[side * modes : (side + 1) * modes], axis=0, keepdims=True)
                spread = pltpu.roll(jnp.broadcast_to(taps, (rows, LANES)), 0, 1, stride=1, stride_axis=0)
                local = jnp.where(causal, spread, 0.0).astype(BF16)[:, :rows]
                halves.append(jnp.dot(local, u, preferred_element_type=F32))
            y_ref[:, columns] = jnp.where(wide_left, halves[0], halves[1])

    @when(stride == 1, is_owner(me))
    def _():
        others = seen_ref.at[pl.ds(0, devices - 1)]
        pltpu.make_async_copy(others, others, recv_sems.at[0]).wait()
        decayed = jnp.exp(-my_decay_ref[...] * float(rows))

        def body(j, carry):
            before_ref[j] = carry.astype(BF16)
            return decayed * carry + seen_ref[j].astype(F32)

        lax.fori_loop(0, devices, body, jnp.zeros(seen_ref.shape[1:], F32))

        @pl.loop(1, devices)
        def _(i):
            other, where = peer(i)
            pltpu.make_async_remote_copy(
                before_ref.at[other],
                carry_ref.at[:, share_of(me // stride)],
                send_sems.at[1],
                recv_sems.at[1],
                device_id=where,
                device_id_type=pl.DeviceIdType.MESH,
            ).start()

        own = pltpu.make_async_copy(before_ref.at[me], carry_ref.at[:, share_of(me // stride)], local_sem)
        own.start()
        own.wait()

    def wait_shares(sem, count):
        some = carry_ref.at[:, pl.ds(0, count * share)]
        pltpu.make_async_copy(some, some, sem).wait()

    if stride == 1:
        wait_shares(send_sems.at[0], owners - 1)
        wait_shares(recv_sems.at[1], owners - 1)
    else:

        @pl.when(is_owner(me))
        def _():
            wait_shares(send_sems.at[0], owners - 1)
            wait_shares(recv_sems.at[1], owners - 1)

        @pl.when(jnp.logical_not(is_owner(me)))
        def _():
            wait_shares(send_sems.at[0], owners)
            wait_shares(recv_sems.at[1], owners)

    after = (lane + 1).astype(F32)
    @pl.loop(0, tiles // UNROLL)
    def _(step):
        for part in range(UNROLL):
            tile = step * UNROLL + part
            columns = cols(tile)
            into = (mode_rows(coef_ref, tile) * jnp.exp(-mode_rows(decay_ref, tile) * after)).astype(BF16)[:, :rows]
            carry = carry_ref[:, columns].astype(F32)
            split = jnp.concatenate([jnp.where(left, carry, 0.0), jnp.where(left, 0.0, carry)], axis=0)
            gained = lax.dot_general(into, split.astype(BF16), (((0,), (0,)), ((), ())), preferred_element_type=F32)
            z = (y_ref[:, columns] + gained).astype(BF16).astype(F32)
            o_ref[:, columns] = (q_ref[:, columns] * z).astype(BF16)

    @when(stride == 1, is_owner(me))
    def _():
        others = before_ref.at[pl.ds(0, devices - 1)]
        pltpu.make_async_copy(others, others, send_sems.at[1]).wait()


def everywhere(block, axis):
    n = lax.axis_size(axis)
    me = lax.axis_index(axis)
    held = [block]
    for shift in range(1, n):
        held.append(lax.ppermute(block, axis, [(i, (i + shift) % n) for i in range(n)]))

    def of(owner):
        shift = lax.rem(me - owner + n, n)
        return lax.select_n(shift == 0, functools.reduce(
            lambda found, s: jnp.where(shift == s, held[s], found), range(1, n), block
        ), block)

    return jnp.concatenate([of(owner) for owner in range(n)], axis=0)


def shards(proj, conv_weight, residues, decays, doc_lengths):
    rows, _, width = proj.shape
    taps = conv_weight.shape[1]
    modes = residues.shape[1]
    devices = lax.axis_size("ctx") * lax.axis_size("mp")
    me = lax.axis_index("ctx") * lax.axis_size("mp") + lax.axis_index("mp")

    x = proj.transpose(1, 0, 2)
    halo = lax.ppermute(x[:, rows - HALO :], AXES, [(i, i + 1) for i in range(devices - 1)])
    both = everywhere(jnp.concatenate([residues, decays], axis=1), "mp")
    residues, decays = both[:, :modes], both[:, modes:]
    groups = residues.shape[0]
    coef = (residues * jnp.sqrt(decays)).reshape(-1, 1)
    coef = jnp.broadcast_to(coef, (groups * modes, LANES))
    decay = jnp.broadcast_to(decays.reshape(-1, 1), (groups * modes, LANES))
    since = rows_since_start(doc_lengths, me * rows + jnp.arange(rows, dtype=jnp.int32))
    mask = (since[None, :] >= jnp.arange(taps)[:, None]).astype(F32)
    mask = jnp.broadcast_to(mask[:, :, None], (taps, rows, LANES))

    mp = lax.axis_size("mp")
    share = max(width // devices, LANES)
    stride = devices * share // width
    channel = (me // stride) * share + jnp.arange(share, dtype=jnp.int32)
    my_decay = jnp.take(decays, channel // (width // groups), axis=0).T
    in_vmem = pl.BlockSpec(memory_space=pltpu.VMEM)
    return pl.pallas_call(
        functools.partial(mixer_kernel, (modes, devices, mp, share, stride)),
        out_shape=jax.ShapeDtypeStruct((rows, width), BF16),
        in_specs=[in_vmem] * 7,
        out_specs=in_vmem,
        scratch_shapes=[
            pltpu.VMEM((rows, width), BF16),
            pltpu.VMEM((rows, width), F32),
            pltpu.VMEM((rows, width), F32),
            pltpu.VMEM((modes, width), BF16),
            pltpu.VMEM((modes, width), BF16),
            pltpu.VMEM((devices, modes, share), BF16),
            pltpu.VMEM((devices, modes, share), BF16),
            pltpu.VMEM((2 * UNROLL, rows + HALO, LANES), F32),
            pltpu.SemaphoreType.DMA,
            pltpu.SemaphoreType.DMA((2,)),
            pltpu.SemaphoreType.DMA((2,)),
        ],
        compiler_params=pltpu.CompilerParams(
            collective_id=0, has_side_effects=True, vmem_limit_bytes=48 * 2**20
        ),
    )(x, halo, conv_weight, mask, decay, coef, my_decay)


def solution(mesh):
    return jax.shard_map(
        shards,
        mesh=mesh,
        in_specs=(P(AXES, None, None), P(), P("mp", None), P("mp", None), P()),
        out_specs=P(AXES, None),
        check_vma=False,
    )
```
